32 devices in a mesh: group: 2 (over x), row: 16 (over z, y, core).
Axes of the slice: x: 2, y: 2, z: 4, core: 2. Of those that a mesh axis runs over, the one named last changes fastest.
Arguments:
- right_side: float32 [16, 393216], P(None, ('group', 'row')), parts along dimension 1, may hold values from -40 to 40
- features: bfloat16 [32, 393216], P(None, ('group', 'row')), parts along dimension 1, may hold values from -3 to 3
- noise: float32 [393216], P(('group', 'row')), parts along dimension 0, may hold values from 0.3 to 3
- clusters: int32 [384], P('group'), parts along dimension 0, may hold values from 0 to 95, never falling along the last dimension, each value on 1 to 8 neighbouring positions
Outputs:
- solution: float32 [16, 393216], P(None, ('group', 'row')), parts along dimension 1
- residual: float32 [16, 393216], P(None, ('group', 'row')), parts along dimension 1
The draws below stay inside these ranges and needn't reach their ends.
There are 2 independent parts, one for each index of `group`. The reference program is written for one: setup_inputs(seed, part) draws one part's arguments, and reference() takes and returns one part's arrays. A program takes and returns all parts, laid end to end along the dimension named above; each array names one. Nothing has to cross between parts.
Inputs may be any that keep to these rules, and one draw needn't show every extreme that they name: clusters[I] is the cluster of row block I; it never falls along the blocks, and each cluster covers 1 to 8 blocks, one exactly 8.
All inputs are finite; a program needn't handle non-finite values.
Results may differ from the reference program's by a relative error of at most 0.0075.
Values may be sent and summed in bfloat16 or wider, within the bound.
A program may use at most 64 MiB of HBM per device.

```python
import math
import jax
import jax.numpy as jnp
import numpy as np
from jax import lax

F = 32
P_SIZE = 16
TILE = 1024
MOSTC = 8
ITERS = 2
HALO = 7
NB = 192
NROWS = 196608


def draw_right_side(key, part):
    key = jax.random.fold_in(key, 11)
    key_base, key_rough = jax.random.split(key, 2)
    position = jnp.arange(NROWS, dtype=jnp.float32) / NROWS
    rising = jnp.exp(math.log(3.0) * position)
    roughness = jnp.exp(jax.random.uniform(key_rough, (NROWS,), jnp.float32, -0.5, 0.5))
    base_vals = jnp.clip(jax.random.normal(key_base, (P_SIZE, NROWS), jnp.float32), -4.0, 4.0)
    values = base_vals * rising[None, :] * roughness[None, :]
    return values


def levels(own_key, shape, pieces, smallest, high):
    factor_of, own = 1.0, jax.random.fold_in(own_key, 6)
    for axis_at, blocks in pieces:
        steps = jnp.exp(jax.random.uniform(jax.random.fold_in(own, axis_at), (blocks,), jnp.float32, smallest / len(pieces), high / len(pieces)))
        factor_of = factor_of * jnp.repeat(steps, shape[axis_at] // blocks).reshape([-1 if axis == axis_at else 1 for axis in range(len(shape))])
    return factor_of


def length_profile(amount, total, limit, slope):
    loads = [(1 << 20) // math.isqrt(standing ** slope) + 1 for standing in range(2, amount + 1)]
    spare, holding = total - limit - (amount - 1), [1] * (amount - 1)
    while spare > 0:
        free = [i for i in range(amount - 1) if holding[i] < limit]
        pool, remaining = sum([loads[i] for i in free]), spare
        for i in free:
            extra = min(limit - holding[i], max(1, remaining * loads[i] // pool), spare)
            holding[i] = holding[i] + extra
            spare = spare - extra
    return np.array([limit] + holding)


def uneven(stream_key, amount, total, limit, skew):
    if amount == 2:
        one = jax.random.randint(stream_key, (), max(1, total - limit), min(limit, total - 1) + 1)
        return jnp.stack([one, total - one])
    lengths = jnp.asarray(length_profile(amount, total, limit, skew), jnp.int32)
    twos = (amount - 1) // 2
    donor, sink = lengths[1:1 + 2 * twos:2], lengths[2:2 + 2 * twos:2]
    margin = jnp.minimum(donor - 1, limit - sink)
    shifted = jax.random.randint(jax.random.fold_in(stream_key, 1), (twos,), 0, 1 << 20) % (margin + 1)
    lengths = lengths.at[1:1 + 2 * twos:2].set(donor - shifted).at[2:2 + 2 * twos:2].set(sink + shifted)
    return lengths[jax.random.permutation(jax.random.fold_in(stream_key, 2), amount)]


def scatter_about(key, shape, scale, reach, cuts=(), kind=jnp.bfloat16):
    result = scale * jax.random.normal(key, shape, jnp.float32)
    if cuts:
        result = result * levels(key, shape, cuts, -0.22, 0.18)
    return jnp.clip(result, -reach, reach).astype(kind)


def setup_inputs(seed: int = 0, part: int = 0) -> dict:
    seeds = jax.random.split(jax.random.key(seed), 5)
    part_splits = jax.random.split(jax.random.fold_in(seeds[4], part), 5)
    return {
        "right_side": draw_right_side(jax.random.fold_in(jax.random.fold_in(seeds[4], part), 71), part),
        "features": scatter_about(part_splits[1], (F, NROWS), 0.6, 3.0, ((1, 16),)),
        "noise": jnp.clip(jnp.exp(math.log(3.0) - 2.3025851 * jax.random.uniform(part_splits[2], (NROWS,), jnp.float32) ** levels(part_splits[2], (NROWS,), ((0, 16),), -0.2, 0.2)), 0.3, 3.0),
        "clusters": jnp.searchsorted(jnp.cumsum(uneven(part_splits[3], NB // 2, NB, MOSTC, 2)), jnp.arange(NB), side="right").astype(jnp.int32),
    }


inv_length = 0.25
amp_factor = 256.0


def kernel_tile(feat_left, feat_right, kernel_scale):
    crossed = lax.dot_general(feat_left, feat_right, (((0,), (0,)), ((), ())), preferred_element_type=jnp.float32)
    left_sq = jnp.sum(jnp.square(feat_left.astype(jnp.float32)), axis=0)
    right_sq = jnp.sum(jnp.square(feat_right.astype(jnp.float32)), axis=0)
    sq_dist = left_sq[:, None] + right_sq[None, :] - 2.0 * crossed
    return (kernel_scale * jnp.exp(-inv_length * sq_dist)).astype(jnp.bfloat16)


def split_parts(vectors):
    high_part = vectors.astype(jnp.bfloat16)
    low_part = (vectors - high_part.astype(vectors.dtype)).astype(jnp.bfloat16)
    return jnp.concatenate([high_part, low_part], axis=0)


def apply_left(tile_vals, parts):
    half = parts.shape[0] // 2
    product = lax.dot_general(parts, tile_vals, (((1,), (1,)), ((), ())), preferred_element_type=jnp.float32)
    return product[:half] + product[half:]


def keep(running):
    return running


def kernel_apply(direction, features, clusters):
    rim_width = HALO * TILE
    parts_pad = jnp.pad(split_parts(direction), ((0, 0), (rim_width, rim_width)))
    feat_pad = jnp.pad(features, ((0, 0), (rim_width, rim_width)))
    blocks = clusters.shape[0]
    kernel_scale = amp_factor / TILE

    def one_block(block_index):
        start_left = ((block_index + HALO) * TILE).astype(jnp.int32)
        feat_left = lax.dynamic_slice_in_dim(feat_pad, start_left, TILE, 1)

        def add_tile(offset, running):
            partner = (block_index + offset - HALO).astype(jnp.int32)
            inside = (partner >= 0) & (partner < blocks)
            matched = clusters[jnp.clip(partner, 0, blocks - 1)] == clusters[block_index]

            def compute(running):
                start = ((block_index + offset) * TILE).astype(jnp.int32)
                feat_right = lax.dynamic_slice_in_dim(feat_pad, start, TILE, 1)
                partner_parts = lax.dynamic_slice_in_dim(parts_pad, start, TILE, 1)
                return running + apply_left(kernel_tile(feat_left, feat_right, kernel_scale), partner_parts)

            return lax.cond(inside & matched, compute, keep, running)

        return lax.fori_loop(0, 2 * HALO + 1, add_tile, jnp.zeros((P_SIZE, TILE), jnp.float32))

    row_blocks = lax.map(one_block, jnp.arange(blocks, dtype=jnp.int32))
    return jnp.transpose(row_blocks, (1, 0, 2)).reshape(P_SIZE, blocks * TILE)


def reference(right_side, features, noise, clusters):
    precond = noise + amp_factor / TILE
    solution = jnp.zeros_like(right_side)
    residual = right_side
    scaled = residual / precond[None, :]
    direction = scaled
    inner_prod = jnp.sum(residual * scaled, axis=1)
    for iteration in range(ITERS):
        applied = kernel_apply(direction, features, clusters) + noise[None, :] * direction
        step_size = inner_prod / jnp.sum(direction * applied, axis=1)
        solution = solution + step_size[:, None] * direction
        residual = residual - step_size[:, None] * applied
        if iteration + 1 < ITERS:
            scaled = residual / precond[None, :]
            inner_next = jnp.sum(residual * scaled, axis=1)
            direction = scaled + (inner_next / inner_prod)[:, None] * direction
            inner_prod = inner_next
    return solution, residual
```

```python
import functools
import math

import jax
import jax.numpy as jnp
from jax import lax
from jax.experimental import pallas as pl
from jax.experimental.pallas import tpu as pltpu
from jax.sharding import PartitionSpec as P

TILE = 1024
MOST = 8
LEFT = 3
RIGHT = 4
CHUNK = 256
CAP = 20
WIDE = 128

inv_length = 0.25
kernel_scale = 256.0 / TILE
log2e = 1.4426950408889634
cross_factor = 2.0 * inv_length * log2e
norm_factor = -inv_length * log2e
log_scale = math.log2(kernel_scale)

f32 = jnp.float32
bf16 = jnp.bfloat16


def three(values):
    one = values.astype(bf16).astype(f32)
    rest = values - one
    two = rest.astype(bf16).astype(f32)
    return one, two, rest - two


def kernel(own, cl, first_ref, feat, rhs, noise, y_out, v_out, dots,
           left_t, right, parts, parts_t, acc, acc_t, tiles):
    total = cl.shape[0]
    first = first_ref[0]
    probes = rhs.shape[0]
    y_out[...] = jnp.zeros_like(y_out)
    v_out[...] = jnp.zeros_like(v_out)
    dots[...] = jnp.zeros_like(dots)

    def columns(block):
        return pl.ds(pl.multiple_of(block * TILE, TILE), TILE)

    def split(k, values):
        high = values.astype(bf16).astype(f32)
        both = jnp.concatenate([high, values - high], axis=0)
        parts[k] = both.astype(bf16)
        parts_t[k] = both.T.astype(bf16)
        acc[k] = jnp.zeros(acc.shape[1:], f32)
        acc_t[k] = jnp.zeros(acc_t.shape[1:], f32)

    def joined(k):
        both = acc[k] + acc_t[k].T
        return both[:probes] + both[probes:]

    def add_dot(at, one, two):
        prod = one * two
        running = prod[:, :WIDE]
        for piece in range(1, TILE // WIDE):
            running = running + prod[:, piece * WIDE:(piece + 1) * WIDE]
        dots[at] = dots[at] + running

    def pair(i, j, slot, fresh, twice):
        below = None
        for c in range(TILE // CHUNK):
            rows = pl.ds(c * CHUNK, CHUNK)
            if fresh:
                power = jnp.dot(left_t[i, rows, :], right[j], preferred_element_type=f32)
                vals = jnp.exp2(power).astype(bf16)
                tiles[slot, rows, :] = vals
            else:
                vals = tiles[slot, rows, :]
            acc_t[i, rows, :] += jnp.dot(vals, parts_t[j], preferred_element_type=f32)
            if twice:
                more = jnp.dot(parts[i, :, rows], vals, preferred_element_type=f32)
                below = more if below is None else below + more
        if twice:
            acc[j] += below

    def all_pairs(length, second):
        def row(i, at):
            def either(j, at, twice):
                slot = jnp.minimum(at, CAP)
                if second:
                    @pl.when(at < CAP)
                    def _():
                        pair(i, j, slot, False, twice)

                    @pl.when(at >= CAP)
                    def _():
                        pair(i, j, slot, True, twice)
                else:
                    pair(i, j, slot, True, twice)
                return at + 1

            at = either(i, at, False)
            return lax.fori_loop(i + 1, length, lambda j, at: either(j, at, True), at)

        lax.fori_loop(0, length, row, jnp.int32(0))

    def cluster(w, length):
        def prepare(k, carry):
            cols = columns(w + k)
            cells = feat[:, cols].astype(f32)
            norm = jnp.sum(cells * cells, axis=0, keepdims=True) * norm_factor
            one, two, rest = three(cells * cross_factor)
            ones = jnp.ones((3, TILE), f32)
            zeros = jnp.zeros((2, TILE), f32)
            tail = jnp.zeros((WIDE - 3 * cells.shape[0] - 8, TILE), f32)
            left = jnp.concatenate(
                [one, two, rest, *three(norm + log_scale), ones, zeros, tail], axis=0)
            left_t[k] = left.T.astype(bf16)
            right[k] = jnp.concatenate(
                [cells, cells, cells, ones, *three(norm), zeros, tail], axis=0).astype(bf16)
            split(k, rhs[:, cols] / (noise[:, cols] + kernel_scale))
            return carry

        def middle(k, carry):
            cols = columns(w + k)
            given = rhs[:, cols]
            precond = noise[:, cols] + kernel_scale
            start = given / precond
            y = joined(k) - kernel_scale * start
            x = y / precond
            y_out[:, cols] = y
            add_dot(0, given, start)
            add_dot(1, start, y)
            add_dot(2, y, x)
            split(k, x)
            return carry

        def finish(k, carry):
            cols = columns(w + k)
            grain = noise[:, cols]
            x = y_out[:, cols] / (grain + kernel_scale)
            v = joined(k) + grain * x
            v_out[:, cols] = v
            add_dot(3, x, v)
            return carry

        lax.fori_loop(0, length, prepare, 0)
        all_pairs(length, False)
        lax.fori_loop(0, length, middle, 0)
        all_pairs(length, True)
        lax.fori_loop(0, length, finish, 0)

    def window(w, carry):
        g = first - LEFT + w
        at = jnp.clip(g, 0, total - 1)
        name = cl[at]
        begins = (g >= 0) & ((g == 0) | (cl[jnp.maximum(at - 1, 0)] != name))
        length = jnp.int32(1)
        for k in range(1, MOST):
            same = (g + k < total) & (cl[jnp.minimum(at + k, total - 1)] == name)
            length = length + same.astype(jnp.int32)
        mid = g + (length - 1) // 2

        @pl.when(begins & (mid >= first) & (mid < first + own))
        def _():
            cluster(w, length)

        return carry

    lax.fori_loop(0, LEFT + own, window, 0)


def extended(cells):
    count = lax.axis_size("row")
    tail = cells[:, cells.shape[1] - LEFT * TILE:]
    head = cells[:, :RIGHT * TILE]
    return jnp.concatenate(
        [
            lax.ppermute(tail, "row", [(i, i + 1) for i in range(count - 1)]),
            cells,
            lax.ppermute(head, "row", [(i + 1, i) for i in range(count - 1)]),
        ],
        axis=1,
    )


def returned(cells):
    count = lax.axis_size("row")
    width = cells.shape[1] - (LEFT + RIGHT) * TILE
    to_left = lax.ppermute(
        cells[:, :LEFT * TILE], "row", [(i + 1, i) for i in range(count - 1)])
    to_right = lax.ppermute(
        cells[:, LEFT * TILE + width:], "row", [(i, i + 1) for i in range(count - 1)])
    mine = cells[:, LEFT * TILE:LEFT * TILE + width]
    return mine + jnp.pad(to_right, ((0, 0), (0, width - RIGHT * TILE))) + jnp.pad(
        to_left, ((0, 0), (width - LEFT * TILE, 0)))


def shards(right_side, features, noise, clusters):
    probes, local = right_side.shape
    own = local // TILE
    feats = features.shape[0]
    span = local + (LEFT + RIGHT) * TILE
    first = (lax.axis_index("row") * own).astype(jnp.int32).reshape(1)
    feat_pad = extended(features)
    values_pad = extended(jnp.concatenate([right_side, noise[None, :]], axis=0))
    rhs_pad = values_pad[:probes]
    noise_pad = values_pad[probes:]
    vmem = pl.BlockSpec(memory_space=pltpu.VMEM)
    smem = pl.BlockSpec(memory_space=pltpu.SMEM)
    y, v, dots = pl.pallas_call(
        functools.partial(kernel, own),
        out_shape=(
            jax.ShapeDtypeStruct((probes, span), f32),
            jax.ShapeDtypeStruct((probes, span), f32),
            jax.ShapeDtypeStruct((4, probes, WIDE), f32),
        ),
        in_specs=[smem, smem, vmem, vmem, vmem],
        out_specs=(vmem, vmem, vmem),
        scratch_shapes=[
            pltpu.VMEM((MOST, TILE, WIDE), bf16),
            pltpu.VMEM((MOST, WIDE, TILE), bf16),
            pltpu.VMEM((MOST, 2 * probes, TILE), bf16),
            pltpu.VMEM((MOST, TILE, 2 * probes), bf16),
            pltpu.VMEM((MOST, 2 * probes, TILE), f32),
            pltpu.VMEM((MOST, TILE, 2 * probes), f32),
            pltpu.VMEM((CAP + 1, TILE, TILE), bf16),
        ],
        compiler_params=pltpu.CompilerParams(vmem_limit_bytes=62 * 1024 * 1024),
    )(clusters, first, feat_pad, rhs_pad, noise_pad)
    a, g, h, k = lax.psum(jnp.sum(dots, axis=2), "row")[:, :, None]
    both = returned(jnp.concatenate([y, v], axis=0))
    y, v = both[:probes], both[probes:]
    base = a + g
    alpha = a / base
    gamma = g / base
    inner_next = alpha * (a * h - g * g) / base
    beta = inner_next / a
    crossed = gamma * base - alpha * (g + h)
    curved = gamma * gamma * base - 2.0 * alpha * gamma * (g + h) + alpha * alpha * k
    step = inner_next / (curved + 2.0 * beta * crossed + beta * beta * base)
    mixed = step * (gamma + beta)
    start = right_side / (noise + kernel_scale)[None, :]
    x = y / (noise + kernel_scale)[None, :]
    solution = (alpha + mixed) * start - (step * alpha) * x
    residual = (gamma - mixed) * right_side - (alpha + mixed) * y + (step * alpha) * v
    return solution, residual


def solution(mesh):
    return jax.shard_map(
        shards,
        mesh=mesh,
        in_specs=(
            P(None, ("group", "row")),
            P(None, ("group", "row")),
            P(("group", "row")),
            P("group"),
        ),
        out_specs=(P(None, ("group", "row")), P(None, ("group", "row"))),
        check_vma=False,
    )
```

```python
import functools
import math

import jax
import jax.numpy as jnp
from jax import lax
from jax.experimental import pallas as pl
from jax.experimental.pallas import tpu as pltpu
from jax.sharding import PartitionSpec as P

TILE = 1024
MOST = 8
LEFT = 7
RIGHT = 7
CHUNK = 256
CAP = 18
WIDE = 128

inv_length = 0.25
kernel_scale = 256.0 / TILE
log2e = 1.4426950408889634
cross_factor = 2.0 * inv_length * log2e
norm_factor = -inv_length * log2e
log_scale = math.log2(kernel_scale)

f32 = jnp.float32
bf16 = jnp.bfloat16


def three(values):
    one = values.astype(bf16).astype(f32)
    rest = values - one
    two = rest.astype(bf16).astype(f32)
    return one, two, rest - two


def kernel(own, total, plan, me_ref, feat, rhs, noise, y_out, v_out, dots,
           left_t, right, parts, parts_t, acc, acc_t, tiles):
    first = me_ref[0] * own
    probes = rhs.shape[0]
    y_out[...] = jnp.zeros_like(y_out)
    v_out[...] = jnp.zeros_like(v_out)
    dots[...] = jnp.zeros_like(dots)

    def columns(block):
        return pl.ds(pl.multiple_of(block * TILE, TILE), TILE)

    def split(k, values):
        high = values.astype(bf16).astype(f32)
        both = jnp.concatenate([high, values - high], axis=0)
        parts[k] = both.astype(bf16)
        parts_t[k] = both.T.astype(bf16)
        acc[k] = jnp.zeros(acc.shape[1:], f32)
        acc_t[k] = jnp.zeros(acc_t.shape[1:], f32)

    def joined(k):
        both = acc[k] + acc_t[k].T
        return both[:probes] + both[probes:]

    def add_dot(at, one, two):
        prod = one * two
        running = prod[:, :WIDE]
        for piece in range(1, TILE // WIDE):
            running = running + prod[:, piece * WIDE:(piece + 1) * WIDE]
        dots[at] = dots[at] + running

    def pair(i, j, slot, fresh, twice):
        below = None
        for c in range(TILE // CHUNK):
            rows = pl.ds(c * CHUNK, CHUNK)
            if fresh:
                power = jnp.dot(left_t[i, rows, :], right[j], preferred_element_type=f32)
                vals = jnp.exp2(power).astype(bf16)
                tiles[slot, rows, :] = vals
            else:
                vals = tiles[slot, rows, :]
            acc_t[i, rows, :] += jnp.dot(vals, parts_t[j], preferred_element_type=f32)
            if twice:
                more = jnp.dot(parts[i, :, rows], vals, preferred_element_type=f32)
                below = more if below is None else below + more
        if twice:
            acc[j] += below

    def all_pairs(length, second):
        def row(i, at):
            def either(j, at, twice):
                slot = jnp.minimum(at, CAP)
                if second:
                    @pl.when(at < CAP)
                    def _():
                        pair(i, j, slot, False, twice)

                    @pl.when(at >= CAP)
                    def _():
                        pair(i, j, slot, True, twice)
                else:
                    pair(i, j, slot, True, twice)
                return at + 1

            at = either(i, at, False)
            return lax.fori_loop(i + 1, length, lambda j, at: either(j, at, True), at)

        lax.fori_loop(0, length, row, jnp.int32(0))

    def cluster(w, length):
        def prepare(k, carry):
            cols = columns(w + k)
            cells = feat[:, cols].astype(f32)
            norm = jnp.sum(cells * cells, axis=0, keepdims=True) * norm_factor
            one, two, rest = three(cells * cross_factor)
            ones = jnp.ones((3, TILE), f32)
            zeros = jnp.zeros((2, TILE), f32)
            tail = jnp.zeros((WIDE - 3 * cells.shape[0] - 8, TILE), f32)
            left = jnp.concatenate(
                [one, two, rest, *three(norm + log_scale), ones, zeros, tail], axis=0)
            left_t[k] = left.T.astype(bf16)
            right[k] = jnp.concatenate(
                [cells, cells, cells, ones, *three(norm), zeros, tail], axis=0).astype(bf16)
            split(k, rhs[:, cols] / (noise[:, cols] + kernel_scale))
            return carry

        def middle(k, carry):
            cols = columns(w + k)
            given = rhs[:, cols]
            precond = noise[:, cols] + kernel_scale
            start = given / precond
            y = joined(k) - kernel_scale * start
            x = y / precond
            y_out[:, cols] = y
            add_dot(0, given, start)
            add_dot(1, start, y)
            add_dot(2, y, x)
            split(k, x)
            return carry

        def finish(k, carry):
            cols = columns(w + k)
            grain = noise[:, cols]
            x = y_out[:, cols] / (grain + kernel_scale)
            v = joined(k) + grain * x
            v_out[:, cols] = v
            add_dot(3, x, v)
            return carry

        lax.fori_loop(0, length, prepare, 0)
        all_pairs(length, False)
        lax.fori_loop(0, length, middle, 0)
        all_pairs(length, True)
        lax.fori_loop(0, length, finish, 0)

    def window(w, carry):
        g = first - LEFT + w
        at = jnp.clip(g, 0, total - 1)

        @pl.when((g >= 0) & (g < total) & (plan[0, at] == me_ref[0]))
        def _():
            cluster(w, plan[1, at])

        return carry

    lax.fori_loop(0, LEFT + own + RIGHT, window, 0)


def planner(count, own, cl, plan):
    total = cl.shape[0]

    def clear(g, carry):
        plan[0, g] = jnp.int32(-1)
        plan[1, g] = jnp.int32(0)
        return carry

    lax.fori_loop(0, total, clear, 0)

    def step(g, carry):
        begin, device, load = carry
        ends = (g == total - 1) | (cl[jnp.minimum(g + 1, total - 1)] != cl[g])
        length = g + 1 - begin
        cost = length * length + length
        bound = own * (device + 1)
        beyond = (device < count - 1) & (g + 1 > bound + RIGHT)
        full = (load + cost > MOST * MOST + MOST) & (begin >= bound - LEFT)
        moved = ends & (device < count - 1) & (beyond | full)
        device = jnp.where(moved, device + 1, device)
        load = jnp.where(moved, 0, load) + jnp.where(ends, cost, 0)

        @pl.when(ends)
        def _():
            plan[0, begin] = device
            plan[1, begin] = length

        return jnp.where(ends, g + 1, begin), device, load

    lax.fori_loop(0, total, step, (jnp.int32(0), jnp.int32(0), jnp.int32(0)))


def extended(cells):
    count = lax.axis_size("row")
    tail = cells[:, cells.shape[1] - LEFT * TILE:]
    head = cells[:, :RIGHT * TILE]
    return jnp.concatenate(
        [
            lax.ppermute(tail, "row", [(i, i + 1) for i in range(count - 1)]),
            cells,
            lax.ppermute(head, "row", [(i + 1, i) for i in range(count - 1)]),
        ],
        axis=1,
    )


def returned(cells):
    count = lax.axis_size("row")
    width = cells.shape[1] - (LEFT + RIGHT) * TILE
    to_left = lax.ppermute(
        cells[:, :LEFT * TILE], "row", [(i + 1, i) for i in range(count - 1)])
    to_right = lax.ppermute(
        cells[:, LEFT * TILE + width:], "row", [(i, i + 1) for i in range(count - 1)])
    mine = cells[:, LEFT * TILE:LEFT * TILE + width]
    return mine + jnp.pad(to_right, ((0, 0), (0, width - RIGHT * TILE))) + jnp.pad(
        to_left, ((0, 0), (width - LEFT * TILE, 0)))


def shards(right_side, features, noise, clusters):
    probes, local = right_side.shape
    own = local // TILE
    feats = features.shape[0]
    span = local + (LEFT + RIGHT) * TILE
    me = lax.axis_index("row").astype(jnp.int32).reshape(1)
    feat_pad = extended(features)
    values_pad = extended(jnp.concatenate([right_side, noise[None, :]], axis=0))
    rhs_pad = values_pad[:probes]
    noise_pad = values_pad[probes:]
    vmem = pl.BlockSpec(memory_space=pltpu.VMEM)
    smem = pl.BlockSpec(memory_space=pltpu.SMEM)
    total = clusters.shape[0]
    plan = pl.pallas_call(
        functools.partial(planner, lax.axis_size("row"), own),
        out_shape=jax.ShapeDtypeStruct((2, total), jnp.int32),
        in_specs=[smem],
        out_specs=smem,
    )(clusters)
    y, v, dots = pl.pallas_call(
        functools.partial(kernel, own, total),
        out_shape=(
            jax.ShapeDtypeStruct((probes, span), f32),
            jax.ShapeDtypeStruct((probes, span), f32),
            jax.ShapeDtypeStruct((4, probes, WIDE), f32),
        ),
        in_specs=[smem, smem, vmem, vmem, vmem],
        out_specs=(vmem, vmem, vmem),
        scratch_shapes=[
            pltpu.VMEM((MOST, TILE, WIDE), bf16),
            pltpu.VMEM((MOST, WIDE, TILE), bf16),
            pltpu.VMEM((MOST, 2 * probes, TILE), bf16),
            pltpu.VMEM((MOST, TILE, 2 * probes), bf16),
            pltpu.VMEM((MOST, 2 * probes, TILE), f32),
            pltpu.VMEM((MOST, TILE, 2 * probes), f32),
            pltpu.VMEM((CAP + 1, TILE, TILE), bf16),
        ],
        compiler_params=pltpu.CompilerParams(vmem_limit_bytes=62 * 1024 * 1024),
    )(plan, me, feat_pad, rhs_pad, noise_pad)
    a, g, h, k = lax.psum(jnp.sum(dots, axis=2), "row")[:, :, None]
    both = returned(jnp.concatenate([y, v], axis=0))
    y, v = both[:probes], both[probes:]
    base = a + g
    alpha = a / base
    gamma = g / base
    inner_next = alpha * (a * h - g * g) / base
    beta = inner_next / a
    crossed = gamma * base - alpha * (g + h)
    curved = gamma * gamma * base - 2.0 * alpha * gamma * (g + h) + alpha * alpha * k
    step = inner_next / (curved + 2.0 * beta * crossed + beta * beta * base)
    mixed = step * (gamma + beta)
    start = right_side / (noise + kernel_scale)[None, :]
    x = y / (noise + kernel_scale)[None, :]
    solution = (alpha + mixed) * start - (step * alpha) * x
    residual = (gamma - mixed) * right_side - (alpha + mixed) * y + (step * alpha) * v
    return solution, residual


def solution(mesh):
    return jax.shard_map(
        shards,
        mesh=mesh,
        in_specs=(
            P(None, ("group", "row")),
            P(None, ("group", "row")),
            P(("group", "row")),
            P("group"),
        ),
        out_specs=(P(None, ("group", "row")), P(None, ("group", "row"))),
        check_vma=False,
    )
```

```python
import functools
import math

import jax
import jax.numpy as jnp
from jax import lax
from jax.experimental import pallas as pl
from jax.experimental.pallas import tpu as pltpu
from jax.sharding import PartitionSpec as P

TILE = 1024
MOST = 8
LEFT = 7
RIGHT = 7
CHUNK = 256
CAP = 18
WIDE = 128

inv_length = 0.25
kernel_scale = 256.0 / TILE
log2e = 1.4426950408889634
cross_factor = 2.0 * inv_length * log2e
norm_factor = -inv_length * log2e
log_scale = math.log2(kernel_scale)

f32 = jnp.float32
bf16 = jnp.bfloat16


def three(values):
    one = values.astype(bf16).astype(f32)
    rest = values - one
    two = rest.astype(bf16).astype(f32)
    return one, two, rest - two


def kernel(own, total, plan, me_ref, feat, rhs, noise, y_out, v_out, dots,
           left_t, right, parts, parts_t, acc, acc_t, tiles):
    first = me_ref[0] * own
    probes = rhs.shape[0]
    y_out[...] = jnp.zeros_like(y_out)
    v_out[...] = jnp.zeros_like(v_out)
    dots[...] = jnp.zeros_like(dots)

    def columns(block):
        return pl.ds(pl.multiple_of(block * TILE, TILE), TILE)

    def split(k, values):
        high = values.astype(bf16).astype(f32)
        both = jnp.concatenate([high, values - high], axis=0)
        parts[k] = both.astype(bf16)
        parts_t[k] = both.T.astype(bf16)
        acc[k] = jnp.zeros(acc.shape[1:], f32)
        acc_t[k] = jnp.zeros(acc_t.shape[1:], f32)

    def joined(k):
        both = acc[k] + acc_t[k].T
        return both[:probes] + both[probes:]

    def add_dot(at, one, two):
        prod = one * two
        running = prod[:, :WIDE]
        for piece in range(1, TILE // WIDE):
            running = running + prod[:, piece * WIDE:(piece + 1) * WIDE]
        dots[at] = dots[at] + running

    def pair(i, j, slot, fresh, twice):
        below = None
        for c in range(TILE // CHUNK):
            rows = pl.ds(c * CHUNK, CHUNK)
            if fresh:
                power = jnp.dot(left_t[i, rows, :], right[j], preferred_element_type=f32)
                vals = jnp.exp2(power).astype(bf16)
                tiles[slot, rows, :] = vals
            else:
                vals = tiles[slot, rows, :]
            if twice:
                acc_t[i, rows, :] += jnp.dot(vals, parts_t[j], preferred_element_type=f32)
            more = jnp.dot(parts[i, :, rows], vals, preferred_element_type=f32)
            below = more if below is None else below + more
        acc[j] += below

    def all_pairs(length, second):
        def row(i, at):
            def either(j, at, twice):
                slot = jnp.minimum(at, CAP)
                if second:
                    @pl.when(at < CAP)
                    def _():
                        pair(i, j, slot, False, twice)

                    @pl.when(at >= CAP)
                    def _():
                        pair(i, j, slot, True, twice)
                else:
                    pair(i, j, slot, True, twice)
                return at + 1

            at = either(i, at, False)
            return lax.fori_loop(i + 1, length, lambda j, at: either(j, at, True), at)

        lax.fori_loop(0, length, row, jnp.int32(0))

    def cluster(w, length):
        def prepare(k, carry):
            cols = columns(w + k)
            cells = feat[:, cols].astype(f32)
            norm = jnp.sum(cells * cells, axis=0, keepdims=True) * norm_factor
            one, two, rest = three(cells * cross_factor)
            ones = jnp.ones((3, TILE), f32)
            zeros = jnp.zeros((2, TILE), f32)
            tail = jnp.zeros((WIDE - 3 * cells.shape[0] - 8, TILE), f32)
            left = jnp.concatenate(
                [one, two, rest, *three(norm + log_scale), ones, zeros, tail], axis=0)
            left_t[k] = left.T.astype(bf16)
            right[k] = jnp.concatenate(
                [cells, cells, cells, ones, *three(norm), zeros, tail], axis=0).astype(bf16)
            split(k, rhs[:, cols] / (noise[:, cols] + kernel_scale))
            return carry

        def middle(k, carry):
            cols = columns(w + k)
            given = rhs[:, cols]
            precond = noise[:, cols] + kernel_scale
            start = given / precond
            y = joined(k) - kernel_scale * start
            x = y / precond
            y_out[:, cols] = y
            add_dot(0, given, start)
            add_dot(1, start, y)
            add_dot(2, y, x)
            split(k, x)
            return carry

        def finish(k, carry):
            cols = columns(w + k)
            grain = noise[:, cols]
            x = y_out[:, cols] / (grain + kernel_scale)
            v = joined(k) + grain * x
            v_out[:, cols] = v
            add_dot(3, x, v)
            return carry

        lax.fori_loop(0, length, prepare, 0)
        all_pairs(length, False)
        lax.fori_loop(0, length, middle, 0)
        all_pairs(length, True)
        lax.fori_loop(0, length, finish, 0)

    def window(w, carry):
        g = first - LEFT + w
        at = jnp.clip(g, 0, total - 1)

        @pl.when((g >= 0) & (g < total) & (plan[0, at] == me_ref[0]))
        def _():
            cluster(w, plan[1, at])

        return carry

    lax.fori_loop(0, LEFT + own + RIGHT, window, 0)


def planner(count, own, cl, plan):
    total = cl.shape[0]

    def clear(g, carry):
        plan[0, g] = jnp.int32(-1)
        plan[1, g] = jnp.int32(0)
        return carry

    lax.fori_loop(0, total, clear, 0)

    def step(g, carry):
        begin, device, load = carry
        ends = (g == total - 1) | (cl[jnp.minimum(g + 1, total - 1)] != cl[g])
        length = g + 1 - begin
        cost = length * length + length
        bound = own * (device + 1)
        beyond = (device < count - 1) & (g + 1 > bound + RIGHT)
        full = (load + cost > MOST * MOST + MOST) & (begin >= bound - LEFT)
        moved = ends & (device < count - 1) & (beyond | full)
        device = jnp.where(moved, device + 1, device)
        load = jnp.where(moved, 0, load) + jnp.where(ends, cost, 0)

        @pl.when(ends)
        def _():
            plan[0, begin] = device
            plan[1, begin] = length

        return jnp.where(ends, g + 1, begin), device, load

    lax.fori_loop(0, total, step, (jnp.int32(0), jnp.int32(0), jnp.int32(0)))


def exchange(count, mine, out, held, send_sem, recv_sem):
    me = lax.axis_index("row")
    barrier = pltpu.get_barrier_semaphore()
    peers = [lax.rem(me + k, count) for k in range(1, count)]
    for peer in peers:
        pl.semaphore_signal(
            barrier, inc=1, device_id={"row": peer}, device_id_type=pl.DeviceIdType.MESH)
    pl.semaphore_wait(barrier, count - 1)
    copies = []
    for k, peer in enumerate(peers):
        copy = pltpu.make_async_remote_copy(
            src_ref=mine,
            dst_ref=held.at[k],
            send_sem=send_sem.at[k],
            recv_sem=recv_sem.at[k],
            device_id={"row": peer},
            device_id_type=pl.DeviceIdType.MESH,
        )
        copy.start()
        copies.append(copy)
    for copy in copies:
        copy.wait()
    total = mine[...]
    for k in range(count - 1):
        total = total + held[k]
    out[...] = total


def summed(values):
    count = lax.axis_size("row")
    vmem = pl.BlockSpec(memory_space=pltpu.VMEM)
    return pl.pallas_call(
        functools.partial(exchange, count),
        out_shape=jax.ShapeDtypeStruct(values.shape, f32),
        in_specs=[vmem],
        out_specs=vmem,
        scratch_shapes=[
            pltpu.VMEM((count - 1,) + values.shape, f32),
            pltpu.SemaphoreType.DMA((count - 1,)),
            pltpu.SemaphoreType.DMA((count - 1,)),
        ],
        compiler_params=pltpu.CompilerParams(collective_id=0, has_side_effects=True),
    )(values)


def extended(cells):
    count = lax.axis_size("row")
    tail = cells[:, cells.shape[1] - LEFT * TILE:]
    head = cells[:, :RIGHT * TILE]
    return jnp.concatenate(
        [
            lax.ppermute(tail, "row", [(i, i + 1) for i in range(count - 1)]),
            cells,
            lax.ppermute(head, "row", [(i + 1, i) for i in range(count - 1)]),
        ],
        axis=1,
    )


def returned(cells):
    count = lax.axis_size("row")
    width = cells.shape[1] - (LEFT + RIGHT) * TILE
    to_left = lax.ppermute(
        cells[:, :LEFT * TILE], "row", [(i + 1, i) for i in range(count - 1)])
    to_right = lax.ppermute(
        cells[:, LEFT * TILE + width:], "row", [(i, i + 1) for i in range(count - 1)])
    mine = cells[:, LEFT * TILE:LEFT * TILE + width]
    return mine + jnp.pad(to_right, ((0, 0), (0, width - RIGHT * TILE))) + jnp.pad(
        to_left, ((0, 0), (width - LEFT * TILE, 0)))


def shards(right_side, features, noise, clusters):
    probes, local = right_side.shape
    own = local // TILE
    feats = features.shape[0]
    span = local + (LEFT + RIGHT) * TILE
    me = lax.axis_index("row").astype(jnp.int32).reshape(1)
    feat_pad = extended(features)
    values_pad = extended(jnp.concatenate([right_side, noise[None, :]], axis=0))
    rhs_pad = values_pad[:probes]
    noise_pad = values_pad[probes:]
    vmem = pl.BlockSpec(memory_space=pltpu.VMEM)
    smem = pl.BlockSpec(memory_space=pltpu.SMEM)
    total = clusters.shape[0]
    plan = pl.pallas_call(
        functools.partial(planner, lax.axis_size("row"), own),
        out_shape=jax.ShapeDtypeStruct((2, total), jnp.int32),
        in_specs=[smem],
        out_specs=smem,
    )(clusters)
    y, v, dots = pl.pallas_call(
        functools.partial(kernel, own, total),
        out_shape=(
            jax.ShapeDtypeStruct((probes, span), f32),
            jax.ShapeDtypeStruct((probes, span), f32),
            jax.ShapeDtypeStruct((4, probes, WIDE), f32),
        ),
        in_specs=[smem, smem, vmem, vmem, vmem],
        out_specs=(vmem, vmem, vmem),
        scratch_shapes=[
            pltpu.VMEM((MOST, TILE, WIDE), bf16),
            pltpu.VMEM((MOST, WIDE, TILE), bf16),
            pltpu.VMEM((MOST, 2 * probes, TILE), bf16),
            pltpu.VMEM((MOST, TILE, 2 * probes), bf16),
            pltpu.VMEM((MOST, 2 * probes, TILE), f32),
            pltpu.VMEM((MOST, TILE, 2 * probes), f32),
            pltpu.VMEM((CAP + 1, TILE, TILE), bf16),
        ],
        compiler_params=pltpu.CompilerParams(vmem_limit_bytes=62 * 1024 * 1024),
    )(plan, me, feat_pad, rhs_pad, noise_pad)
    sums = jnp.pad(jnp.sum(dots, axis=2), ((0, 4), (0, WIDE - probes)))
    a, g, h, k = summed(sums)[:4, :probes, None]
    both = returned(jnp.concatenate([y, v], axis=0))
    y, v = both[:probes], both[probes:]
    base = a + g
    alpha = a / base
    gamma = g / base
    inner_next = alpha * (a * h - g * g) / base
    beta = inner_next / a
    crossed = gamma * base - alpha * (g + h)
    curved = gamma * gamma * base - 2.0 * alpha * gamma * (g + h) + alpha * alpha * k
    step = inner_next / (curved + 2.0 * beta * crossed + beta * beta * base)
    mixed = step * (gamma + beta)
    start = right_side / (noise + kernel_scale)[None, :]
    x = y / (noise + kernel_scale)[None, :]
    solution = (alpha + mixed) * start - (step * alpha) * x
    residual = (gamma - mixed) * right_side - (alpha + mixed) * y + (step * alpha) * v
    return solution, residual


def solution(mesh):
    return jax.shard_map(
        shards,
        mesh=mesh,
        in_specs=(
            P(None, ("group", "row")),
            P(None, ("group", "row")),
            P(("group", "row")),
            P("group"),
        ),
        out_specs=(P(None, ("group", "row")), P(None, ("group", "row"))),
        check_vma=False,
    )
```
